512 devices in a mesh: cell: 32 (over x, y, core), gene: 16 (over z).
Axes of the slice: x: 4, y: 4, z: 16, core: 2. Of those that a mesh axis runs over, the one named last changes fastest.
Arguments:
- counts: int32 [8192, 8192], P('cell', 'gene'), may hold values from 0 to 83, as said below
- prior_basis: float32 [8192, 128], P('gene'), may hold values from -0.0625 to 0.0625
- prior_values: float32 [128], replicated, may hold values from 0.3 to 1.5
Outputs:
- loadings: float32 [8192, 128], P('gene')
- scores: float32 [8192, 128], P('cell')
The draws below stay inside these ranges and needn't reach their ends.
Inputs may be any that keep to these rules, and one draw needn't show every extreme that they name: `counts`: every cell has a nonzero count in at least one gene.
All inputs are finite; a program needn't handle non-finite values.
Results may differ from the reference program's by a relative error of at most 0.0003.
Values sent between devices are 32-bit elements; how exact they have to be, the bound alone decides.
A program may use at most 64 MiB of HBM per device.

```python
import math
import jax
import jax.numpy as jnp
from jax import lax

G = 8192
K = 128
ITERS = 3
CELLS = 8192


def draw_counts(key, part):
    key_gene, key_cell, key_value = jax.random.split(key, 3)
    gene_index = lax.broadcasted_iota(jnp.int32, (CELLS, G), 1)
    cell_index = lax.broadcasted_iota(jnp.int32, (CELLS, G), 0)
    level = 2 + 6 * gene_index // G
    gene_factor = jax.random.randint(key_gene, (1, G), 1, 4)
    cell_factor = jax.random.randint(key_cell, (CELLS, 1), 1, 5)
    ceiling = level * gene_factor * cell_factor
    values = jax.random.randint(key_value, (CELLS, G), 0, ceiling)
    anchor = (gene_index == cell_index % G).astype(jnp.int32)
    return jnp.minimum(values + anchor, 83)


def levels(rng, dims, shards, low, high):
    level, own = 1.0, jax.random.fold_in(rng, 6)
    for dim, parts in shards:
        heights = jnp.exp(jax.random.uniform(jax.random.fold_in(own, dim), (parts,), jnp.float32, low / len(shards), high / len(shards)))
        level = level * jnp.repeat(heights, dims[dim] // parts).reshape([-1 if axis == dim else 1 for axis in range(len(dims))])
    return level


def noise(key, extent, width, limit, shards=(), dtype=jnp.bfloat16):
    drawn = jax.random.normal(key, extent, jnp.float32) * width
    if len(shards) > 0:
        drawn = levels(key, extent, shards, -0.22, 0.18) * drawn
    return jnp.clip(drawn, min=-limit, max=limit).astype(dtype)


def setup_inputs(seed: int = 0) -> dict:
    arg_keys = jax.random.split(jax.random.key(seed), 4)
    return {
        "counts": draw_counts(jax.random.fold_in(arg_keys[3], 71), 0),
        "prior_basis": noise(arg_keys[1], (G, K), G ** -0.5, 0.0625, ((0, 16),), jnp.float32),
        "prior_values": jnp.clip(jnp.exp(jax.random.uniform(arg_keys[2], (K,), jnp.float32, math.log(0.3), math.log(1.5))), 0.3, 1.5),
    }


scale_factor = 10000.0

def reference(counts, prior_basis, prior_values):
    highest = lax.Precision.HIGHEST
    expression = counts.astype(jnp.float32)
    library = lax.optimization_barrier(jnp.sum(expression, axis=1, keepdims=True))
    expression = jnp.log1p(scale_factor * expression / library)
    centered = expression - lax.optimization_barrier(jnp.mean(expression, axis=0))
    weights = prior_values * prior_values
    basis = prior_basis
    for step in range(ITERS):
        projected = jnp.dot(centered.astype(jnp.float32), basis.astype(jnp.float32), precision=highest, preferred_element_type=jnp.float32)
        image = lax.dot_general(centered.astype(jnp.float32), projected.astype(jnp.float32), (((0,), (0,)), ((), ())), precision=highest, preferred_element_type=jnp.float32) / jnp.float32(CELLS)
        correlation = lax.dot_general(prior_basis.astype(jnp.float32), basis.astype(jnp.float32), (((0,), (0,)), ((), ())), precision=highest, preferred_element_type=jnp.float32)
        image = image + jnp.dot(prior_basis.astype(jnp.float32), (weights[:, None] * correlation).astype(jnp.float32), precision=highest, preferred_element_type=jnp.float32)
        gram = lax.dot_general(image.astype(jnp.float32), image.astype(jnp.float32), (((0,), (0,)), ((), ())), precision=highest, preferred_element_type=jnp.float32)
        lower = jnp.linalg.cholesky(gram)
        basis = lax.linalg.triangular_solve(lower, image, left_side=False, lower=True, transpose_a=True)
    scores = jnp.dot(centered.astype(jnp.float32), basis.astype(jnp.float32), precision=highest, preferred_element_type=jnp.float32)
    return (jnp.sqrt(jnp.float32(G)) * basis, scores)
```

```python
import functools

import jax
import jax.numpy as jnp
from jax import lax
from jax.experimental import pallas as pl
from jax.experimental.pallas import tpu as pltpu
from jax.sharding import PartitionSpec as P

ITERS = 3
SCALE = 10000.0
HIGHEST = lax.Precision.HIGHEST
MESH = pl.DeviceIdType.MESH
F32 = jnp.float32

LIB, MEAN, SHIFT, GRAM, RSZ, AGZ, RSC, AGC = range(8)

SLOT = 24
PANEL = 32


def dot(left, right, dims):
    return lax.dot_general(left, right, (dims, ((), ())), precision=HIGHEST, preferred_element_type=F32)


NN = ((1,), (0,))
NT = ((1,), (1,))
TN = ((0,), (0,))


def factor_panel(step, s_ref, w_ref):
    k = s_ref.shape[0]
    upper, lower = s_ref[0:PANEL, :], w_ref[0:PANEL, :]
    sub = lax.broadcasted_iota(jnp.int32, (PANEL, 1), 0)
    for i in range(PANEL):
        ratio = jnp.where(sub > i, upper[:, i : i + 1] / upper[i : i + 1, i : i + 1], 0.0)
        upper, lower = upper - ratio * upper[i : i + 1, :], lower - ratio * lower[i : i + 1, :]
    lane = lax.broadcasted_iota(jnp.int32, (PANEL, k), 1)
    row = lax.broadcasted_iota(jnp.int32, (PANEL, k), 0)
    pivots = jnp.sum(jnp.where(lane == row, upper, 0.0), axis=1, keepdims=True)
    scale = 1.0 / jnp.sqrt(pivots)
    upper, lower = upper * scale, lower * scale
    ahead = jnp.where((lane >= PANEL) & (lane < k - PANEL * step), upper, 0.0)
    s_new = s_ref[PANEL:k, :] - dot(ahead, upper, TN)[PANEL:k, :]
    w_new = w_ref[PANEL:k, :] - dot(ahead, lower, TN)[PANEL:k, :]
    s_ref[0 : k - PANEL, :] = pltpu.roll(s_new, k - PANEL, 1)
    s_ref[k - PANEL : k, :] = upper
    w_ref[0 : k - PANEL, :] = w_new
    w_ref[k - PANEL : k, :] = lower


def kernel(
    ng, nc, counts_ref, prior_ref, values_ref, load_ref, score_ref,
    x_ref, xt_ref, ysend, yrecv, ychunk, yfull, lsend, lrecv, msend, mrecv, dsend, drecv,
    gsend, grecv, isend, irecv, ichunk, ifull, s_ref, w_ref, send_sem, recv_sem,
):
    cell, gene = lax.axis_index("cell"), lax.axis_index("gene")
    rows, cols = counts_ref.shape
    k = prior_ref.shape[1]
    part = rows // ng
    own = cols // nc
    grow = k // nc
    total = rows * nc

    def copy(kind, src, dst, where):
        return pltpu.make_async_remote_copy(
            src_ref=src, dst_ref=dst, send_sem=send_sem.at[kind], recv_sem=recv_sem.at[kind],
            device_id=where, device_id_type=MESH,
        )

    def to_genes(kind, src, dst):
        def send(target):
            copy(kind, src(target), dst, {"gene": target}).start()

        send((gene + ng // 2) % ng)

        def both(i, carry):
            send((gene + ng // 2 + i) % ng)
            send((gene + ng // 2 - i) % ng)
            return carry

        lax.fori_loop(1, ng // 2, both, 0)

    def to_cells(kind, src, dst):
        def send(i, carry):
            target = (cell + i) % nc
            copy(kind, src(target), dst, {"cell": target}).start()
            return carry

        lax.fori_loop(1, nc, send, 0)

    def take(kind, ref):
        copy(kind, ref, ref, {"gene": (gene + 1) % ng}).wait_recv()

    def sent(kind, ref):
        copy(kind, ref, ref, {"gene": (gene + 1) % ng}).wait_send()

    barrier = pltpu.get_barrier_semaphore()

    def greet_gene(i, carry):
        pl.semaphore_signal(barrier, 1, device_id={"gene": (gene + i) % ng}, device_id_type=MESH)
        return carry

    def greet_cell(i, carry):
        pl.semaphore_signal(barrier, 1, device_id={"cell": (cell + i) % nc}, device_id_type=MESH)
        return carry

    lax.fori_loop(1, ng, greet_gene, 0)
    lax.fori_loop(1, nc, greet_cell, 0)

    counts = counts_ref[...].astype(F32)
    lsend[...] = dot(jnp.ones((8, cols), F32), counts, NT)
    prior = prior_ref[...]
    pick = lax.broadcasted_iota(jnp.int32, (ng, k), 1) == lax.broadcasted_iota(jnp.int32, (ng, k), 0) + cell * ng
    prior_rows = dot(jnp.where(pick, 1.0, 0.0) * values_ref[...], prior, NT)
    x_ref[...] = jnp.zeros_like(x_ref)
    yfull[...] = jnp.zeros_like(yfull)
    for g in range(ng):
        x_ref[g, part : part + 1, :] = prior_rows[g : g + 1, :]

    pl.semaphore_wait(barrier, ng + nc - 2)

    to_genes(LIB, lambda t: lsend.at[pl.ds(0, 1)], lrecv.at[gene, pl.ds(0, 1)])
    lrecv[gene, 0:1, :] = lsend[0:1, :]
    take(LIB, lrecv.at[pl.ds(0, ng - 1), pl.ds(0, 1)])
    library = jnp.broadcast_to(jnp.sum(lrecv[:, 0:1, :], axis=0), (8, rows))
    factor = SCALE / dot(library, jnp.full((8, 128), 0.125, F32), TN)
    means = []
    for b in range(cols // 128):
        expression = jnp.log1p(counts[:, 128 * b : 128 * (b + 1)] * factor)
        mean = jnp.mean(expression, axis=0, keepdims=True)
        means.append(mean)
        x_ref[:, 0:part, 128 * b : 128 * (b + 1)] = (expression - mean).reshape(ng, part, 128)
    local_mean = jnp.concatenate(means, axis=1)
    msend[0:1, :] = local_mean
    to_cells(MEAN, lambda t: msend.at[pl.ds(0, 1)], mrecv.at[cell, pl.ds(0, 1)])
    mrecv[cell, 0:1, :] = local_mean

    lane8 = lax.broadcasted_iota(jnp.int32, (8, k), 1)
    row8 = lax.broadcasted_iota(jnp.int32, (8, k), 0)
    gram_pick = jnp.where((lane8 == row8 + cell * grow) & (row8 < grow), 1.0, 0.0)
    iota_s = lax.broadcasted_iota(jnp.int32, (k, k), 0)
    eye = jnp.where(iota_s == lax.broadcasted_iota(jnp.int32, (k, k), 1), 1.0, 0.0)

    for step in range(ITERS + 1):
        rsz_rows = part + 1 + (grow if step > 0 else 0)
        image = prior if step == 0 else ifull[...]
        y = dot(x_ref[...].reshape(ng * SLOT, cols), image, NN)
        if step > 0:
            sent(RSZ, ysend.at[pl.ds(0, ng - 1), pl.ds(0, rsz_prev)])
        ysend[...] = y.reshape(ng, SLOT, k)
        if step > 0:
            gram_rows = dot(dot(gram_pick, image, NT), image, NN)
            for g in range(ng):
                ysend[g, part + 1 : part + 1 + grow, :] = gram_rows[0:grow, :]
        to_genes(RSZ, lambda t: ysend.at[t, pl.ds(0, rsz_rows)], yrecv.at[gene, pl.ds(0, rsz_rows)])
        yrecv[gene] = ysend[gene]
        if step == 0:
            take(MEAN, mrecv.at[pl.ds(0, nc - 1), pl.ds(0, 1)])
            delta = local_mean - jnp.sum(mrecv[:, 0:1, :], axis=0) * (1.0 / nc)
            dsend[...] = dot(jnp.broadcast_to(delta, (8, cols)), prior, NN)
            to_genes(SHIFT, lambda t: dsend.at[pl.ds(0, 1)], drecv.at[gene, pl.ds(0, 1)])
            drecv[gene, 0:1, :] = dsend[0:1, :]
            x_ref[:, 0:part, :] = x_ref[:, 0:part, :] + delta[None]
        take(RSZ, yrecv.at[pl.ds(0, ng - 1), pl.ds(0, rsz_rows)])
        chunk = jnp.sum(yrecv[...], axis=0)
        if step > 0:
            sent(AGZ, yfull.at[pl.ds(0, ng - 1), pl.ds(0, part + 1)])
        ychunk[...] = chunk
        to_genes(AGZ, lambda t: ychunk.at[pl.ds(0, part + 1)], yfull.at[gene, pl.ds(0, part + 1)])
        yfull[gene, 0 : part + 1, :] = chunk[0 : part + 1, :]
        if step > 0:
            if step > 1:
                sent(GRAM, grecv.at[pl.ds(0, nc - 1), pl.ds(0, grow)])
            gsend[0:grow, :] = chunk[part + 1 : part + 1 + grow, :]
            to_cells(GRAM, lambda t: gsend.at[pl.ds(0, grow)], grecv.at[cell, pl.ds(0, grow)])
            grecv[cell, 0:grow, :] = gsend[0:grow, :]
        else:
            lanes = lax.broadcasted_iota(jnp.int32, (1, ng * SLOT), 1)
            xt_ref[...] = x_ref[...].reshape(ng * SLOT, cols).T * jnp.where(lanes % SLOT < part, 1.0 / total, 1.0)
            take(SHIFT, drecv.at[pl.ds(0, ng - 1), pl.ds(0, 1)])
        if step == ITERS:
            take(GRAM, grecv.at[pl.ds(0, nc - 1), pl.ds(0, grow)])
            for c in range(nc):
                s_ref[c * grow : (c + 1) * grow, :] = grecv[c, 0:grow, :]
            w_ref[...] = eye
            lax.fori_loop(0, k // PANEL, lambda i, a: (factor_panel(i, s_ref, w_ref), a)[1], 0)
            inverse = w_ref[...]
            load_ref[...] = dot(image, inverse, NT) * jnp.sqrt(F32(cols * ng))
        take(AGZ, yfull.at[pl.ds(0, ng - 1), pl.ds(0, part + 1)])
        if step == ITERS:
            score_ref[...] = dot(yfull[:, 0:part, :].reshape(rows, k), inverse, NT)
            break
        if step == 0:
            yfull[:, 0:part, :] = yfull[:, 0:part, :] + jnp.sum(drecv[:, 0:1, :], axis=0)[None]
        partial = dot(xt_ref[...], yfull[...].reshape(ng * SLOT, k), NN)
        if step > 0:
            sent(RSC, irecv.at[pl.ds(0, nc - 1)])
        isend[...] = partial.reshape(nc, own, k)
        to_cells(RSC, lambda t: isend.at[t], irecv.at[cell])
        irecv[cell] = isend[cell]
        if step > 0:
            take(GRAM, grecv.at[pl.ds(0, nc - 1), pl.ds(0, grow)])
            for c in range(nc):
                s_ref[c * grow : (c + 1) * grow, :] = grecv[c, 0:grow, :]
            w_ref[...] = eye
            lax.fori_loop(0, 2, lambda i, a: (factor_panel(i, s_ref, w_ref), a)[1], 0)
        take(RSC, irecv.at[pl.ds(0, nc - 1)])
        mine = jnp.sum(irecv[...], axis=0)
        if step > 0:
            sent(AGC, ifull.at[pl.ds(0, (nc - 1) * own)])
        ichunk[...] = mine
        place = pl.ds(pl.multiple_of(cell * own, own), own)
        to_cells(AGC, lambda t: ichunk, ifull.at[place])
        ifull[place, :] = mine
        if step > 0:
            lax.fori_loop(2, k // PANEL, lambda i, a: (factor_panel(i, s_ref, w_ref), a)[1], 0)
        take(AGC, ifull.at[pl.ds(0, (nc - 1) * own)])
        if step > 0:
            ifull[...] = dot(ifull[...], w_ref[...], NT)
        rsz_prev = rsz_rows

    sent(LIB, lrecv.at[pl.ds(0, ng - 1), pl.ds(0, 1)])
    sent(MEAN, mrecv.at[pl.ds(0, nc - 1), pl.ds(0, 1)])
    sent(SHIFT, drecv.at[pl.ds(0, ng - 1), pl.ds(0, 1)])
    sent(GRAM, grecv.at[pl.ds(0, nc - 1), pl.ds(0, grow)])
    sent(RSZ, ysend.at[pl.ds(0, ng - 1), pl.ds(0, rsz_rows)])
    sent(AGZ, yfull.at[pl.ds(0, ng - 1), pl.ds(0, part + 1)])
    sent(RSC, irecv.at[pl.ds(0, nc - 1)])
    sent(AGC, ifull.at[pl.ds(0, (nc - 1) * own)])


def solution(mesh):
    ng, nc = mesh.shape["gene"], mesh.shape["cell"]

    def per_device(counts, prior_basis, prior_values):
        rows, cols = counts.shape
        k = prior_basis.shape[1]
        part, own = rows // ng, cols // nc
        vmem = pl.BlockSpec(memory_space=pltpu.VMEM)
        scratch = [
            (ng, SLOT, cols), (cols, ng * SLOT),
            (ng, SLOT, k), (ng, SLOT, k), (SLOT, k), (ng, SLOT, k),
            (8, rows), (ng, 8, rows),
            (8, cols), (nc, 8, cols),
            (8, k), (ng, 8, k),
            (8, k), (nc, 8, k),
            (nc, own, k), (nc, own, k), (own, k), (cols, k),
            (k, k), (k, k),
        ]
        return pl.pallas_call(
            functools.partial(kernel, ng, nc),
            out_shape=(jax.ShapeDtypeStruct((cols, k), F32), jax.ShapeDtypeStruct((rows, k), F32)),
            in_specs=[vmem] * 3,
            out_specs=(vmem, vmem),
            scratch_shapes=[pltpu.VMEM(s, F32) for s in scratch]
            + [pltpu.SemaphoreType.DMA((8,)), pltpu.SemaphoreType.DMA((8,))],
            compiler_params=pltpu.CompilerParams(
                collective_id=0, has_side_effects=True, vmem_limit_bytes=40 * 2**20
            ),
        )(counts, prior_basis, prior_values.reshape(1, k))

    return jax.shard_map(
        per_device,
        mesh=mesh,
        in_specs=(P("cell", "gene"), P("gene", None), P()),
        out_specs=(P("gene", None), P("cell", None)),
        check_vma=False,
    )
```

```python
import functools

import jax
import jax.numpy as jnp
from jax import lax
from jax.experimental import pallas as pl
from jax.experimental.pallas import tpu as pltpu
from jax.sharding import PartitionSpec as P

ITERS = 3
SCALE = 10000.0
HIGHEST = lax.Precision.HIGHEST
MESH = pl.DeviceIdType.MESH
F32 = jnp.float32

LIB, MEAN, SHIFT, RSZ, AGZ, RSC, AGC, GRAM_C, GRAM_Z, GRAM = range(10)

SLOT = 24
PANEL, BLOCK = 32, 8


def dot(left, right, dims):
    return lax.dot_general(left, right, (dims, ((), ())), precision=HIGHEST, preferred_element_type=F32)


NN = ((1,), (0,))
NT = ((1,), (1,))
TN = ((0,), (0,))


def split(value):
    high = value.astype(jnp.bfloat16)
    rest = value - high.astype(F32)
    middle = rest.astype(jnp.bfloat16)
    return high, middle, (rest - middle.astype(F32)).astype(jnp.bfloat16)


def product(parts, right):
    n = right.shape[1]
    high, middle, low = split(right)
    wide = jnp.concatenate([high, middle], axis=1)

    def mxu(a, b):
        return jnp.dot(a, b, preferred_element_type=F32)

    first, second = mxu(parts[0][...], wide), mxu(parts[1][...], wide)
    small = mxu(parts[2][...], high) + mxu(parts[0][...], low) + second[:, n:]
    return first[:, :n] + (first[:, n:] + second[:, :n] + small)


def factor_panel(step, s_ref, w_ref):
    k = s_ref.shape[0]
    upper, lower = s_ref[0:PANEL, :], w_ref[0:PANEL, :]
    sub = lax.broadcasted_iota(jnp.int32, (PANEL, k), 0)
    lane = lax.broadcasted_iota(jnp.int32, (PANEL, k), 1)
    for b in range(0, PANEL, BLOCK):
        columns = [jnp.broadcast_to(upper[:, b + j : b + j + 1], (PANEL, k)) for j in range(BLOCK)]
        for j in range(BLOCK):
            i = b + j
            ratio = jnp.where(sub > i, columns[j] * (1.0 / columns[j][i : i + 1, :]), 0.0)
            for later in range(j + 1, BLOCK):
                columns[later] = columns[later] - ratio * columns[later][i : i + 1, :]
            upper = upper - ratio * upper[i : i + 1, :]
            lower = lower - ratio * lower[i : i + 1, :]
    pivots = jnp.sum(jnp.where(lane == sub, upper, 0.0), axis=1, keepdims=True)
    scale = 1.0 / jnp.sqrt(pivots)
    upper, lower = upper * scale, lower * scale
    ahead = jnp.where((lane >= PANEL) & (lane < k - PANEL * step), upper, 0.0)
    change = dot(ahead, jnp.concatenate([upper, lower], axis=1), TN)
    s_ref[0 : k - PANEL, :] = pltpu.roll(s_ref[PANEL:k, :] - change[PANEL:k, 0:k], k - PANEL, 1)
    w_new = w_ref[PANEL:k, :] - change[PANEL:k, k : 2 * k]
    s_ref[k - PANEL : k, :] = upper
    w_ref[0 : k - PANEL, :] = w_new
    w_ref[k - PANEL : k, :] = lower


def kernel(
    ng, nc, counts_hbm, prior_hbm, values_hbm, load_ref, score_ref,
    counts_ref, prior_ref, values_ref,
    x_ref, ysend, yrecv, ychunk, yfull, lsend, lrecv, msend, mrecv, dsend, drecv,
    gsend, grecv, zsend, zrecv, csend, crecv, isend, irecv, ichunk, ifull, s_ref, w_ref,
    x_high, x_middle, x_low, t_high, t_middle, t_low, send_sem, recv_sem, load_sem,
):
    cell, gene = lax.axis_index("cell"), lax.axis_index("gene")
    rows, cols = counts_ref.shape
    k = prior_ref.shape[1]
    part = rows // ng
    own = cols // nc
    grow = k // nc
    total = rows * nc
    x_parts, t_parts = (x_high, x_middle, x_low), (t_high, t_middle, t_low)

    loads = [
        pltpu.make_async_copy(src, dst, load_sem.at[i])
        for i, (src, dst) in enumerate(
            [(counts_hbm, counts_ref), (prior_hbm, prior_ref), (values_hbm, values_ref)]
        )
    ]
    for load in loads:
        load.start()

    def copy(kind, src, dst, where):
        return pltpu.make_async_remote_copy(
            src_ref=src, dst_ref=dst, send_sem=send_sem.at[kind], recv_sem=recv_sem.at[kind],
            device_id=where, device_id_type=MESH,
        )

    def to_genes(kind, src, dst):
        def send(target):
            copy(kind, src(target), dst, {"gene": target}).start()

        send(lax.rem(gene + ng // 2, ng))

        def both(i, carry):
            send(lax.rem(gene + ng // 2 + i, ng))
            send(lax.rem(gene + ng // 2 - i + ng, ng))
            return carry

        lax.fori_loop(1, ng // 2, both, 0)

    core = lax.rem(cell, 2)
    chip_y = lax.rem(lax.div(cell, 2), 4)
    chip_x = lax.div(cell, 8)

    def turn(i):
        half = lax.div(i, 2)
        return lax.rem(2 + 3 * i + half * (3 + 2 * lax.rem(i, 2)), 4)

    def to_cells(kind, src, dst):
        def send(i, carry):
            x = lax.rem(chip_x + turn(lax.div(i, 8)), 4)
            y = lax.rem(chip_y + turn(lax.rem(lax.div(i, 2), 4)), 4)
            target = x * 8 + y * 2 + lax.rem(core + 1 + i, 2)
            copy(kind, src(target), dst, {"cell": target}).start()
            return carry

        lax.fori_loop(0, nc - 1, send, 0)

    def take(kind, ref):
        copy(kind, ref, ref, {"gene": lax.rem(gene + 1, ng)}).wait_recv()

    def sent(kind, ref):
        copy(kind, ref, ref, {"gene": lax.rem(gene + 1, ng)}).wait_send()

    weight = {
        LIB: lrecv.at[pl.ds(0, ng - 1), pl.ds(0, 1)],
        MEAN: mrecv.at[pl.ds(0, nc - 1), pl.ds(0, 1)],
        SHIFT: drecv.at[pl.ds(0, ng - 1), pl.ds(0, 1)],
        RSZ: yrecv.at[pl.ds(0, ng - 1), pl.ds(0, part + 1)],
        AGZ: yfull.at[pl.ds(0, ng - 1), pl.ds(0, part + 1)],
        RSC: irecv.at[pl.ds(0, nc - 1)],
        AGC: ifull.at[pl.ds(0, (nc - 1) * own)],
        GRAM_C: grecv.at[pl.ds(0, nc - 1)],
        GRAM_Z: zrecv.at[pl.ds(0, ng - 1)],
        GRAM: crecv.at[pl.ds(0, nc - 1)],
    }

    barrier = pltpu.get_barrier_semaphore()

    def greet_gene(i, carry):
        pl.semaphore_signal(barrier, 1, device_id={"gene": lax.rem(gene + i, ng)}, device_id_type=MESH)
        return carry

    def greet_cell(i, carry):
        pl.semaphore_signal(barrier, 1, device_id={"cell": lax.rem(cell + i, nc)}, device_id_type=MESH)
        return carry

    lax.fori_loop(1, ng, greet_gene, 0)
    lax.fori_loop(1, nc, greet_cell, 0)

    loads[0].wait()
    counts = counts_ref[...].astype(F32)
    lsend[...] = lax.dot_general(
        jnp.ones((8, cols), jnp.bfloat16), counts.astype(jnp.bfloat16), (NT, ((), ())), preferred_element_type=F32
    )
    loads[1].wait()
    loads[2].wait()
    prior = prior_ref[...]
    pick = lax.broadcasted_iota(jnp.int32, (ng, k), 1) == lax.broadcasted_iota(jnp.int32, (ng, k), 0) + cell * ng
    prior_rows = dot(jnp.where(pick, 1.0, 0.0) * values_ref[...], prior, NT)
    x_ref[...] = jnp.zeros_like(x_ref)
    yfull[...] = jnp.zeros_like(yfull)
    for g in range(ng):
        x_ref[g, part : part + 1, :] = prior_rows[g : g + 1, :]

    pl.semaphore_wait(barrier, ng + nc - 2)

    to_genes(LIB, lambda t: lsend.at[pl.ds(0, 1)], lrecv.at[gene, pl.ds(0, 1)])
    lrecv[gene, 0:1, :] = lsend[0:1, :]
    take(LIB, weight[LIB])
    library = jnp.broadcast_to(jnp.sum(lrecv[:, 0:1, :], axis=0), (8, rows))
    factor = SCALE / dot(library, jnp.full((8, 128), 0.125, F32), TN)
    means = []
    for b in range(cols // 128):
        expression = jnp.log1p(counts_ref[:, 128 * b : 128 * (b + 1)].astype(F32) * factor)
        mean = jnp.mean(expression, axis=0, keepdims=True)
        means.append(mean)
        x_ref[:, 0:part, 128 * b : 128 * (b + 1)] = (expression - mean).reshape(ng, part, 128)
    local_mean = jnp.concatenate(means, axis=1)
    msend[0:1, :] = local_mean
    to_cells(MEAN, lambda t: msend.at[pl.ds(0, 1)], mrecv.at[cell, pl.ds(0, 1)])
    mrecv[cell, 0:1, :] = local_mean

    place = pl.ds(pl.multiple_of(cell * own, own), own)

    def scatter_genes(y):
        ysend[...] = y.reshape(ng, SLOT, k)
        to_genes(RSZ, lambda t: ysend.at[t, pl.ds(0, part + 1)], yrecv.at[gene, pl.ds(0, part + 1)])
        yrecv[gene] = ysend[gene]

    def gather_genes():
        take(RSZ, weight[RSZ])
        ychunk[...] = jnp.sum(yrecv[...], axis=0)
        to_genes(AGZ, lambda t: ychunk.at[pl.ds(0, part + 1)], yfull.at[gene, pl.ds(0, part + 1)])
        yfull[gene, 0 : part + 1, :] = ychunk[0 : part + 1, :]

    def scatter_cells():
        isend[...] = product(t_parts, yfull[...].reshape(ng * SLOT, k)).reshape(nc, own, k)
        to_cells(RSC, lambda t: isend.at[t], irecv.at[cell])
        irecv[cell] = isend[cell]

    def gather_cells(mine):
        ichunk[...] = mine
        to_cells(AGC, lambda t: ichunk, ifull.at[place])
        ifull[place, :] = mine
        gram = dot(mine, mine, TN)
        for c in range(nc):
            gsend[c] = gram[c * grow : (c + 1) * grow, :]
        to_cells(GRAM_C, lambda t: gsend.at[t], grecv.at[cell])
        grecv[cell] = gsend[cell]

    def gram_genes():
        take(GRAM_C, weight[GRAM_C])
        zsend[...] = jnp.sum(grecv[...], axis=0)
        to_genes(GRAM_Z, lambda t: zsend, zrecv.at[gene])
        zrecv[gene] = zsend[...]

    def gram_cells():
        take(GRAM_Z, weight[GRAM_Z])
        csend[...] = jnp.sum(zrecv[...], axis=0)
        to_cells(GRAM, lambda t: csend, crecv.at[cell])
        crecv[cell] = csend[...]

    def factorise():
        take(GRAM, weight[GRAM])
        for c in range(nc):
            s_ref[c * grow : (c + 1) * grow, :] = crecv[c]
        w_ref[...] = jnp.where(
            lax.broadcasted_iota(jnp.int32, (k, k), 0) == lax.broadcasted_iota(jnp.int32, (k, k), 1), 1.0, 0.0
        )

        def panel(i, carry):
            factor_panel(i, s_ref, w_ref)
            return carry

        lax.fori_loop(0, k // PANEL, panel, 0)

    scatter_genes(dot(x_ref[...].reshape(ng * SLOT, cols), prior, NN))
    take(MEAN, weight[MEAN])
    delta = local_mean - jnp.sum(mrecv[:, 0:1, :], axis=0) * (1.0 / nc)
    dsend[...] = dot(jnp.broadcast_to(delta, (8, cols)), prior, NN)
    to_genes(SHIFT, lambda t: dsend.at[pl.ds(0, 1)], drecv.at[gene, pl.ds(0, 1)])
    drecv[gene, 0:1, :] = dsend[0:1, :]
    x_ref[:, 0:part, :] = x_ref[:, 0:part, :] + delta[None]
    gather_genes()
    x = x_ref[...].reshape(ng * SLOT, cols)
    for ref, value in zip(x_parts, split(x)):
        ref[...] = value
    lanes = lax.broadcasted_iota(jnp.int32, (1, ng * SLOT), 1)
    for ref, value in zip(t_parts, split(x.T * jnp.where(lanes % SLOT < part, 1.0 / total, 1.0))):
        ref[...] = value
    take(SHIFT, weight[SHIFT])
    take(AGZ, weight[AGZ])
    yfull[:, 0:part, :] = yfull[:, 0:part, :] + jnp.sum(drecv[:, 0:1, :], axis=0)[None]
    scatter_cells()
    sent(RSZ, weight[RSZ])
    sent(AGZ, weight[AGZ])
    take(RSC, weight[RSC])
    gather_cells(jnp.sum(irecv[...], axis=0))

    def to_basis():
        gram_genes()
        take(AGC, weight[AGC])
        scatter_genes(product(x_parts, ifull[...]))
        gram_cells()
        gather_genes()
        factorise()

    def iteration(step, carry):
        to_basis()
        take(AGZ, weight[AGZ])
        sent(RSC, weight[RSC])
        scatter_cells()
        for kind in (RSZ, AGZ, AGC, GRAM_C, GRAM_Z, GRAM):
            sent(kind, weight[kind])
        take(RSC, weight[RSC])
        gather_cells(dot(jnp.sum(irecv[...], axis=0), w_ref[...], NT))
        return carry

    lax.fori_loop(1, ITERS, iteration, 0)

    to_basis()
    load_ref[...] = dot(ifull[...], w_ref[...], NT) * jnp.sqrt(F32(cols * ng))
    take(AGZ, weight[AGZ])
    score_ref[...] = dot(yfull[:, 0:part, :].reshape(rows, k), w_ref[...], NT)
    for kind in (LIB, MEAN, SHIFT, RSC, RSZ, AGZ, AGC, GRAM_C, GRAM_Z, GRAM):
        sent(kind, weight[kind])


def solution(mesh):
    ng, nc = mesh.shape["gene"], mesh.shape["cell"]

    def per_device(counts, prior_basis, prior_values):
        rows, cols = counts.shape
        k = prior_basis.shape[1]
        part, own = rows // ng, cols // nc
        grow = k // nc
        vmem, hbm = pl.BlockSpec(memory_space=pltpu.VMEM), pl.BlockSpec(memory_space=pltpu.HBM)
        scratch = [
            (cols, k), (1, k),
            (ng, SLOT, cols),
            (ng, SLOT, k), (ng, SLOT, k), (SLOT, k), (ng, SLOT, k),
            (8, rows), (ng, 8, rows),
            (8, cols), (nc, 8, cols),
            (8, k), (ng, 8, k),
            (nc, grow, k), (nc, grow, k), (grow, k), (ng, grow, k), (grow, k), (nc, grow, k),
            (nc, own, k), (nc, own, k), (own, k), (cols, k),
            (k, k), (k, k),
        ]
        return pl.pallas_call(
            functools.partial(kernel, ng, nc),
            out_shape=(jax.ShapeDtypeStruct((cols, k), F32), jax.ShapeDtypeStruct((rows, k), F32)),
            in_specs=[hbm] * 3,
            out_specs=(vmem, vmem),
            scratch_shapes=[pltpu.VMEM((rows, cols), jnp.int32)]
            + [pltpu.VMEM(s, F32) for s in scratch]
            + [pltpu.VMEM((ng * SLOT, cols), jnp.bfloat16)] * 3
            + [pltpu.VMEM((cols, ng * SLOT), jnp.bfloat16)] * 3
            + [pltpu.SemaphoreType.DMA((10,)), pltpu.SemaphoreType.DMA((10,)), pltpu.SemaphoreType.DMA((3,))],
            compiler_params=pltpu.CompilerParams(
                collective_id=0, has_side_effects=True, vmem_limit_bytes=56_000_000
            ),
        )(counts, prior_basis, prior_values.reshape(1, k))

    return jax.shard_map(
        per_device,
        mesh=mesh,
        in_specs=(P("cell", "gene"), P("gene", None), P()),
        out_specs=(P("gene", None), P("cell", None)),
        check_vma=False,
    )
```

```python
import functools

import jax
import jax.numpy as jnp
from jax import lax
from jax.experimental import pallas as pl
from jax.experimental.pallas import tpu as pltpu
from jax.sharding import PartitionSpec as P

ITERS = 3
SCALE = 10000.0
HIGHEST = lax.Precision.HIGHEST
MESH = pl.DeviceIdType.MESH
F32 = jnp.float32

KINDS = 11
LIB, MEAN, SHIFT, RSZ, AGZ, RSC, AGC, GRAM_C, GRAM, GRAM_Z, _ = range(KINDS)

SLOT = 24
PANEL, BLOCK = 32, 8


def dot(left, right, dims):
    return lax.dot_general(left, right, (dims, ((), ())), precision=HIGHEST, preferred_element_type=F32)


NN = ((1,), (0,))
NT = ((1,), (1,))
TN = ((0,), (0,))


def split(value):
    high = value.astype(jnp.bfloat16)
    rest = value - high.astype(F32)
    middle = rest.astype(jnp.bfloat16)
    return high, middle, (rest - middle.astype(F32)).astype(jnp.bfloat16)


def product(parts, right):
    n = right.shape[1]
    high, middle, low = split(right)
    wide = jnp.concatenate([high, middle], axis=1)

    def mxu(a, b):
        return jnp.dot(a, b, preferred_element_type=F32)

    first, second = mxu(parts[0][...], wide), mxu(parts[1][...], wide)
    small = mxu(parts[2][...], high) + mxu(parts[0][...], low) + second[:, n:]
    return first[:, :n] + (first[:, n:] + second[:, :n] + small)


def factor_panel(step, s_ref, w_ref, last=False):
    k = s_ref.shape[0]
    upper, lower = s_ref[0:PANEL, :], w_ref[0:PANEL, :]
    sub = lax.broadcasted_iota(jnp.int32, (PANEL, k), 0)
    lane = lax.broadcasted_iota(jnp.int32, (PANEL, k), 1)
    for b in range(0, PANEL, BLOCK):
        columns = [jnp.broadcast_to(upper[:, b + j : b + j + 1], (PANEL, k)) for j in range(BLOCK)]
        for j in range(BLOCK):
            i = b + j
            ratio = jnp.where(sub > i, columns[j] * (1.0 / columns[j][i : i + 1, :]), 0.0)
            for later in range(j + 1, BLOCK):
                columns[later] = columns[later] - ratio * columns[later][i : i + 1, :]
            upper = upper - ratio * upper[i : i + 1, :]
            lower = lower - ratio * lower[i : i + 1, :]
    pivots = jnp.sum(jnp.where(lane == sub, upper, 0.0), axis=1, keepdims=True)
    scale = 1.0 / jnp.sqrt(pivots)
    upper, lower = upper * scale, lower * scale
    if last:
        w_ref[0 : k - PANEL, :] = w_ref[PANEL:k, :]
        w_ref[k - PANEL : k, :] = lower
        return
    ahead = jnp.where((lane >= PANEL) & (lane < k - PANEL * step), upper, 0.0)
    change = dot(ahead, jnp.concatenate([upper, lower], axis=1), TN)
    s_ref[0 : k - PANEL, :] = pltpu.roll(s_ref[PANEL:k, :] - change[PANEL:k, 0:k], k - PANEL, 1)
    w_new = w_ref[PANEL:k, :] - change[PANEL:k, k : 2 * k]
    s_ref[k - PANEL : k, :] = upper
    w_ref[0 : k - PANEL, :] = w_new
    w_ref[k - PANEL : k, :] = lower


def kernel(
    ng, nc, counts_hbm, prior_hbm, values_hbm, load_ref, score_ref,
    counts_ref, prior_ref, values_ref,
    x_ref, ysend, yrecv, ychunk, yfull, lsend, lrecv, msend, mrecv, dsend, drecv,
    gsend, grecv, zsend, zrecv, csend, crecv, isend, irecv, ichunk, ifull, s_ref, w_ref,
    x_high, x_middle, x_low, t_high, t_middle, t_low, send_sem, recv_sem, load_sem,
):
    cell, gene = lax.axis_index("cell"), lax.axis_index("gene")
    rows, cols = counts_ref.shape
    k = prior_ref.shape[1]
    part = rows // ng
    own = cols // nc
    grow = k // nc
    total = rows * nc
    x_parts, t_parts = (x_high, x_middle, x_low), (t_high, t_middle, t_low)

    loads = [
        pltpu.make_async_copy(src, dst, load_sem.at[i])
        for i, (src, dst) in enumerate(
            [(counts_hbm, counts_ref), (prior_hbm, prior_ref), (values_hbm, values_ref)]
        )
    ]
    for load in loads:
        load.start()

    def copy(kind, src, dst, where):
        return pltpu.make_async_remote_copy(
            src_ref=src, dst_ref=dst, send_sem=send_sem.at[kind], recv_sem=recv_sem.at[kind],
            device_id=where, device_id_type=MESH,
        )

    def genes(act):
        act(lax.rem(gene + ng // 2, ng))

        def both(i, carry):
            act(lax.rem(gene + ng // 2 + i, ng))
            act(lax.rem(gene + ng // 2 - i + ng, ng))
            return carry

        lax.fori_loop(1, ng // 2, both, 0, unroll=True)

    core = lax.rem(cell, 2)
    chip_y = lax.rem(lax.div(cell, 2), 4)
    chip_x = lax.div(cell, 8)

    def turn(i):
        half = lax.div(i, 2)
        return lax.rem(2 + 3 * i + half * (3 + 2 * lax.rem(i, 2)), 4)

    def cells(act):
        def one(i, carry):
            x = lax.rem(chip_x + turn(lax.div(i, 8)), 4)
            y = lax.rem(chip_y + turn(lax.rem(lax.div(i, 2), 4)), 4)
            act(x * 8 + y * 2 + lax.rem(core + 1 + i, 2))
            return carry

        lax.fori_loop(0, nc - 1, one, 0, unroll=True)

    def to_genes(kind, src, dst):
        genes(lambda target: copy(kind, src(target), dst, {"gene": target}).start())

    def to_cells(kind, src, dst):
        cells(lambda target: copy(kind, src(target), dst, {"cell": target}).start())

    def take(kind, ref):
        copy(kind, ref, ref, {"gene": lax.rem(gene + 1, ng)}).wait_recv()

    def sent(kind, ref):
        copy(kind, ref, ref, {"gene": lax.rem(gene + 1, ng)}).wait_send()

    weight = {
        LIB: lrecv.at[pl.ds(0, ng - 1), pl.ds(0, 1)],
        MEAN: mrecv.at[pl.ds(0, nc - 1), pl.ds(0, 1)],
        SHIFT: drecv.at[pl.ds(0, ng - 1), pl.ds(0, 1)],
        RSC: irecv.at[pl.ds(0, nc - 1)],
        AGC: ifull.at[pl.ds(0, (nc - 1) * own)],
        GRAM_C: grecv.at[pl.ds(0, nc - 1)],
        GRAM: crecv.at[pl.ds(0, nc - 1)],
    }

    barrier = pltpu.get_barrier_semaphore()

    genes(lambda t: pl.semaphore_signal(barrier, 1, device_id={"gene": t}, device_id_type=MESH))
    cells(lambda t: pl.semaphore_signal(barrier, 1, device_id={"cell": t}, device_id_type=MESH))

    loads[0].wait()
    counts = counts_ref[...].astype(F32)
    lsend[...] = lax.dot_general(
        jnp.ones((8, cols), jnp.bfloat16), counts.astype(jnp.bfloat16), (NT, ((), ())), preferred_element_type=F32
    )
    loads[1].wait()
    loads[2].wait()
    prior = prior_ref[...]
    pick = lax.broadcasted_iota(jnp.int32, (ng, k), 1) == lax.broadcasted_iota(jnp.int32, (ng, k), 0) + cell * ng
    prior_rows = dot(jnp.where(pick, 1.0, 0.0) * values_ref[...], prior, NT)
    x_ref[...] = jnp.zeros_like(x_ref)
    yfull[...] = jnp.zeros_like(yfull)
    for g in range(ng):
        x_ref[g, part : part + 1, :] = prior_rows[g : g + 1, :]

    pl.semaphore_wait(barrier, ng + nc - 2)

    to_genes(LIB, lambda t: lsend.at[pl.ds(0, 1)], lrecv.at[gene, pl.ds(0, 1)])
    lrecv[gene, 0:1, :] = lsend[0:1, :]
    take(LIB, weight[LIB])
    library = jnp.broadcast_to(jnp.sum(lrecv[:, 0:1, :], axis=0), (8, rows))
    factor = SCALE / dot(library, jnp.full((8, 128), 0.125, F32), TN)
    means = []
    for b in range(cols // 128):
        expression = jnp.log1p(counts_ref[:, 128 * b : 128 * (b + 1)].astype(F32) * factor)
        mean = jnp.mean(expression, axis=0, keepdims=True)
        means.append(mean)
        x_ref[:, 0:part, 128 * b : 128 * (b + 1)] = (expression - mean).reshape(ng, part, 128)
    local_mean = jnp.concatenate(means, axis=1)
    msend[0:1, :] = local_mean
    to_cells(MEAN, lambda t: msend.at[pl.ds(0, 1)], mrecv.at[cell, pl.ds(0, 1)])
    mrecv[cell, 0:1, :] = local_mean

    place = pl.ds(pl.multiple_of(cell * own, own), own)

    def scatter_genes(n):
        to_genes(RSZ, lambda t: ysend.at[t, pl.ds(0, n)], yrecv.at[gene, pl.ds(0, n)])
        yrecv[gene] = ysend[gene]

    def gather_genes(n):
        take(RSZ, yrecv.at[pl.ds(0, ng - 1), pl.ds(0, n)])
        ychunk[0:n, :] = jnp.sum(yrecv[:, 0:n, :], axis=0)
        to_genes(AGZ, lambda t: ychunk.at[pl.ds(0, n)], yfull.at[gene, pl.ds(0, n)])
        yfull[gene, 0:n, :] = ychunk[0:n, :]

    def take_genes(n):
        take(AGZ, yfull.at[pl.ds(0, ng - 1), pl.ds(0, n)])

    def sent_genes(n):
        sent(RSZ, yrecv.at[pl.ds(0, ng - 1), pl.ds(0, n)])
        sent(AGZ, yfull.at[pl.ds(0, ng - 1), pl.ds(0, n)])

    def scatter_cells():
        isend[...] = product(t_parts, yfull[...].reshape(ng * SLOT, k)).reshape(nc, own, k)
        to_cells(RSC, lambda t: isend.at[t], irecv.at[cell])
        irecv[cell] = isend[cell]

    def gather_cells(mine):
        ichunk[...] = mine
        to_cells(AGC, lambda t: ichunk, ifull.at[place])
        ifull[place, :] = mine
        gram = dot(mine, mine, TN)
        for c in range(nc):
            gsend[c] = gram[c * grow : (c + 1) * grow, :]
        to_cells(GRAM_C, lambda t: gsend.at[t], grecv.at[cell])
        grecv[cell] = gsend[cell]

    def gram_genes(turn):
        take(GRAM_C, weight[GRAM_C])
        zsend[...] = jnp.sum(grecv[...], axis=0)
        to_genes(GRAM_Z + turn, lambda t: zsend, zrecv.at[turn, gene])
        zrecv[turn, gene] = zsend[...]

    def gram_cells(turn):
        take(GRAM_Z + turn, zrecv.at[turn, pl.ds(0, ng - 1)])
        csend[...] = jnp.sum(zrecv[turn], axis=0)
        to_cells(GRAM, lambda t: csend, crecv.at[cell])
        crecv[cell] = csend[...]

    def factorise():
        take(GRAM, weight[GRAM])
        for c in range(nc):
            s_ref[c * grow : (c + 1) * grow, :] = crecv[c]
        w_ref[...] = jnp.where(
            lax.broadcasted_iota(jnp.int32, (k, k), 0) == lax.broadcasted_iota(jnp.int32, (k, k), 1), 1.0, 0.0
        )

        def panel(i, carry):
            factor_panel(i, s_ref, w_ref)
            return carry

        lax.fori_loop(0, k // PANEL - 1, panel, 0)
        factor_panel(k // PANEL - 1, s_ref, w_ref, last=True)

    ysend[...] = dot(x_ref[...].reshape(ng * SLOT, cols), prior, NN).reshape(ng, SLOT, k)
    scatter_genes(part + 1)
    take(MEAN, weight[MEAN])
    delta = local_mean - jnp.sum(mrecv[:, 0:1, :], axis=0) * (1.0 / nc)
    dsend[...] = dot(jnp.broadcast_to(delta, (8, cols)), prior, NN)
    to_genes(SHIFT, lambda t: dsend.at[pl.ds(0, 1)], drecv.at[gene, pl.ds(0, 1)])
    drecv[gene, 0:1, :] = dsend[0:1, :]
    x_ref[:, 0:part, :] = x_ref[:, 0:part, :] + delta[None]
    gather_genes(part + 1)
    x = x_ref[...].reshape(ng * SLOT, cols)
    for ref, value in zip(x_parts, split(x)):
        ref[...] = value
    lanes = lax.broadcasted_iota(jnp.int32, (1, ng * SLOT), 1)
    for ref, value in zip(t_parts, split(x.T * jnp.where(lanes % SLOT < part, 1.0 / total, 1.0))):
        ref[...] = value
    take(SHIFT, weight[SHIFT])
    take_genes(part + 1)
    yfull[:, 0:part, :] = yfull[:, 0:part, :] + jnp.sum(drecv[:, 0:1, :], axis=0)[None]
    scatter_cells()
    sent_genes(part + 1)
    take(RSC, weight[RSC])
    gather_cells(jnp.sum(irecv[...], axis=0))

    def to_products():
        take(AGC, weight[AGC])
        ysend[...] = product(x_parts, ifull[...]).reshape(ng, SLOT, k)

    def iteration(step, carry):
        side = lax.rem(step, 2)
        to_products()
        scatter_genes(part + 1)
        gram_genes(side)
        gather_genes(part + 1)
        gram_cells(side)
        take_genes(part + 1)
        sent(RSC, weight[RSC])
        scatter_cells()
        factorise()
        sent_genes(part + 1)
        for kind in (AGC, GRAM_C, GRAM):
            sent(kind, weight[kind])
        sent(GRAM_Z + side, zrecv.at[side, pl.ds(0, ng - 1)])
        take(RSC, weight[RSC])
        gather_cells(dot(jnp.sum(irecv[...], axis=0), w_ref[...], NT))
        return carry

    lax.fori_loop(1, ITERS, iteration, 0)

    to_products()
    last = ITERS % 2
    gram_genes(last)
    scatter_genes(part)
    gram_cells(last)
    gather_genes(part)
    factorise()
    load_ref[...] = dot(ifull[...], w_ref[...], NT) * jnp.sqrt(F32(cols * ng))
    take_genes(part)
    score_ref[...] = dot(yfull[:, 0:part, :].reshape(rows, k), w_ref[...], NT)
    sent_genes(part)
    sent(GRAM_Z + last, zrecv.at[last, pl.ds(0, ng - 1)])
    for kind in (LIB, MEAN, SHIFT, RSC, AGC, GRAM_C, GRAM):
        sent(kind, weight[kind])


def solution(mesh):
    ng, nc = mesh.shape["gene"], mesh.shape["cell"]

    def per_device(counts, prior_basis, prior_values):
        rows, cols = counts.shape
        k = prior_basis.shape[1]
        part, own = rows // ng, cols // nc
        grow = k // nc
        vmem, hbm = pl.BlockSpec(memory_space=pltpu.VMEM), pl.BlockSpec(memory_space=pltpu.HBM)
        scratch = [
            (cols, k), (1, k),
            (ng, SLOT, cols),
            (ng, SLOT, k), (ng, SLOT, k), (SLOT, k), (ng, SLOT, k),
            (8, rows), (ng, 8, rows),
            (8, cols), (nc, 8, cols),
            (8, k), (ng, 8, k),
            (nc, grow, k), (nc, grow, k), (grow, k), (2, ng, grow, k), (grow, k), (nc, grow, k),
            (nc, own, k), (nc, own, k), (own, k), (cols, k),
            (k, k), (k, k),
        ]
        return pl.pallas_call(
            functools.partial(kernel, ng, nc),
            out_shape=(jax.ShapeDtypeStruct((cols, k), F32), jax.ShapeDtypeStruct((rows, k), F32)),
            in_specs=[hbm] * 3,
            out_specs=(vmem, vmem),
            scratch_shapes=[pltpu.VMEM((rows, cols), jnp.int32)]
            + [pltpu.VMEM(s, F32) for s in scratch]
            + [pltpu.VMEM((ng * SLOT, cols), jnp.bfloat16)] * 3
            + [pltpu.VMEM((cols, ng * SLOT), jnp.bfloat16)] * 3
            + [pltpu.SemaphoreType.DMA((KINDS,)), pltpu.SemaphoreType.DMA((KINDS,)), pltpu.SemaphoreType.DMA((3,))],
            compiler_params=pltpu.CompilerParams(
                collective_id=0, has_side_effects=True, vmem_limit_bytes=56_000_000
            ),
        )(counts, prior_basis, prior_values.reshape(1, k))

    return jax.shard_map(
        per_device,
        mesh=mesh,
        in_specs=(P("cell", "gene"), P("gene", None), P()),
        out_specs=(P("gene", None), P("cell", None)),
        check_vma=False,
    )
```

```python
import functools

import jax
import jax.numpy as jnp
from jax import lax
from jax.experimental import pallas as pl
from jax.experimental.pallas import tpu as pltpu
from jax.sharding import PartitionSpec as P

ITERS = 3
SCALE = 10000.0
HIGHEST = lax.Precision.HIGHEST
MESH = pl.DeviceIdType.MESH
F32 = jnp.float32

KINDS = 11
LIB, MEAN, SHIFT, RSZ, AGZ, RSC, AGC, GRAM_C, GRAM, GRAM_Z, _ = range(KINDS)

SLOT = 24
PANEL, BLOCK = 32, 8


def dot(left, right, dims):
    return lax.dot_general(left, right, (dims, ((), ())), precision=HIGHEST, preferred_element_type=F32)


NN = ((1,), (0,))
NT = ((1,), (1,))
TN = ((0,), (0,))


def split(value):
    high = value.astype(jnp.bfloat16)
    rest = value - high.astype(F32)
    middle = rest.astype(jnp.bfloat16)
    return high, middle, (rest - middle.astype(F32)).astype(jnp.bfloat16)


def product(parts, right):
    n = right.shape[1]
    high, middle, low = split(right)
    wide = jnp.concatenate([high, middle], axis=1)

    def mxu(a, b):
        return jnp.dot(a, b, preferred_element_type=F32)

    first, second = mxu(parts[0][...], wide), mxu(parts[1][...], wide)
    small = mxu(parts[2][...], high) + mxu(parts[0][...], low) + second[:, n:]
    return first[:, :n] + (first[:, n:] + second[:, :n] + small)


def factor_panel(step, s_ref, w_ref, last=False):
    k = s_ref.shape[0]
    upper, lower = s_ref[0:PANEL, :], w_ref[0:PANEL, :]
    sub = lax.broadcasted_iota(jnp.int32, (PANEL, k), 0)
    lane = lax.broadcasted_iota(jnp.int32, (PANEL, k), 1)
    for b in range(0, PANEL, BLOCK):
        columns = [jnp.broadcast_to(upper[:, b + j : b + j + 1], (PANEL, k)) for j in range(BLOCK)]
        for j in range(BLOCK):
            i = b + j
            ratio = jnp.where(sub > i, columns[j] * (1.0 / columns[j][i : i + 1, :]), 0.0)
            for later in range(j + 1, BLOCK):
                columns[later] = columns[later] - ratio * columns[later][i : i + 1, :]
            upper = upper - ratio * upper[i : i + 1, :]
            lower = lower - ratio * lower[i : i + 1, :]
    pivots = jnp.sum(jnp.where(lane == sub, upper, 0.0), axis=1, keepdims=True)
    scale = 1.0 / jnp.sqrt(pivots)
    upper, lower = upper * scale, lower * scale
    if last:
        w_ref[0 : k - PANEL, :] = w_ref[PANEL:k, :]
        w_ref[k - PANEL : k, :] = lower
        return
    ahead = jnp.where((lane >= PANEL) & (lane < k - PANEL * step), upper, 0.0)
    change = dot(ahead, jnp.concatenate([upper, lower], axis=1), TN)
    s_ref[0 : k - PANEL, :] = pltpu.roll(s_ref[PANEL:k, :] - change[PANEL:k, 0:k], k - PANEL, 1)
    w_new = w_ref[PANEL:k, :] - change[PANEL:k, k : 2 * k]
    s_ref[k - PANEL : k, :] = upper
    w_ref[0 : k - PANEL, :] = w_new
    w_ref[k - PANEL : k, :] = lower


def kernel(
    ng, nc, counts_hbm, prior_hbm, values_hbm, load_ref, score_ref,
    counts_ref, prior_ref, values_ref,
    x_ref, ysend, yrecv, ychunk, yfull, lsend, lrecv, msend, mrecv, dsend, drecv,
    gsend, grecv, zsend, zrecv, csend, crecv, isend, irecv, ichunk, ifull, s_ref, w_ref,
    x_high, x_middle, x_low, t_high, t_middle, t_low, send_sem, recv_sem, load_sem,
):
    cell, gene = lax.axis_index("cell"), lax.axis_index("gene")
    rows, cols = counts_ref.shape
    k = prior_ref.shape[1]
    part = rows // ng
    own = cols // nc
    grow = k // nc
    total = rows * nc
    x_parts, t_parts = (x_high, x_middle, x_low), (t_high, t_middle, t_low)

    loads = [
        pltpu.make_async_copy(src, dst, load_sem.at[i])
        for i, (src, dst) in enumerate(
            [(counts_hbm, counts_ref), (prior_hbm, prior_ref), (values_hbm, values_ref)]
        )
    ]
    for load in loads:
        load.start()

    def copy(kind, src, dst, where):
        return pltpu.make_async_remote_copy(
            src_ref=src, dst_ref=dst, send_sem=send_sem.at[kind], recv_sem=recv_sem.at[kind],
            device_id=where, device_id_type=MESH,
        )

    def genes(act):
        act(lax.rem(gene + ng // 2, ng))

        def both(i, carry):
            act(lax.rem(gene + ng // 2 + i, ng))
            act(lax.rem(gene + ng // 2 - i + ng, ng))
            return carry

        lax.fori_loop(1, ng // 2, both, 0, unroll=True)

    core = lax.rem(cell, 2)
    chip_y = lax.rem(lax.div(cell, 2), 4)
    chip_x = lax.div(cell, 8)

    def turn(i):
        half = lax.div(i, 2)
        return lax.rem(2 + 3 * i + half * (3 + 2 * lax.rem(i, 2)), 4)

    def cells(act):
        def one(i, carry):
            x = lax.rem(chip_x + turn(lax.div(i, 8)), 4)
            y = lax.rem(chip_y + turn(lax.rem(lax.div(i, 2), 4)), 4)
            act(x * 8 + y * 2 + lax.rem(core + 1 + i, 2))
            return carry

        lax.fori_loop(0, nc - 1, one, 0, unroll=True)

    def to_genes(kind, src, dst):
        genes(lambda target: copy(kind, src(target), dst, {"gene": target}).start())

    def to_cells(kind, src, dst):
        cells(lambda target: copy(kind, src(target), dst, {"cell": target}).start())

    def take(kind, ref):
        copy(kind, ref, ref, {"gene": lax.rem(gene + 1, ng)}).wait_recv()

    def sent(kind, ref):
        copy(kind, ref, ref, {"gene": lax.rem(gene + 1, ng)}).wait_send()

    weight = {
        LIB: lrecv.at[pl.ds(0, ng - 1), pl.ds(0, 1)],
        MEAN: mrecv.at[pl.ds(0, nc - 1), pl.ds(0, 1)],
        SHIFT: drecv.at[pl.ds(0, ng - 1), pl.ds(0, 1)],
        RSC: irecv.at[pl.ds(0, nc - 1)],
        AGC: ifull.at[pl.ds(0, (nc - 1) * own)],
        GRAM_C: grecv.at[pl.ds(0, nc - 1)],
        GRAM: crecv.at[pl.ds(0, nc - 1)],
    }

    barrier = pltpu.get_barrier_semaphore()

    genes(lambda t: pl.semaphore_signal(barrier, 1, device_id={"gene": t}, device_id_type=MESH))
    cells(lambda t: pl.semaphore_signal(barrier, 1, device_id={"cell": t}, device_id_type=MESH))

    loads[0].wait()
    counts = counts_ref[...].astype(F32)
    lsend[...] = lax.dot_general(
        jnp.ones((8, cols), jnp.bfloat16), counts.astype(jnp.bfloat16), (NT, ((), ())), preferred_element_type=F32
    )
    loads[1].wait()
    loads[2].wait()
    prior = prior_ref[...]
    pick = lax.broadcasted_iota(jnp.int32, (ng, k), 1) == lax.broadcasted_iota(jnp.int32, (ng, k), 0) + cell * ng
    prior_rows = dot(jnp.where(pick, 1.0, 0.0) * values_ref[...], prior, NT)
    x_ref[...] = jnp.zeros_like(x_ref)
    yfull[...] = jnp.zeros_like(yfull)
    for g in range(ng):
        x_ref[g, part : part + 1, :] = prior_rows[g : g + 1, :]

    pl.semaphore_wait(barrier, ng + nc - 2)

    to_genes(LIB, lambda t: lsend.at[pl.ds(0, 1)], lrecv.at[gene, pl.ds(0, 1)])
    lrecv[gene, 0:1, :] = lsend[0:1, :]
    take(LIB, weight[LIB])
    library = jnp.broadcast_to(jnp.sum(lrecv[:, 0:1, :], axis=0), (8, rows))
    factor = SCALE / dot(library, jnp.full((8, 128), 0.125, F32), TN)
    means = []
    for b in range(cols // 128):
        expression = jnp.log1p(counts_ref[:, 128 * b : 128 * (b + 1)].astype(F32) * factor)
        mean = jnp.mean(expression, axis=0, keepdims=True)
        means.append(mean)
        x_ref[:, 0:part, 128 * b : 128 * (b + 1)] = (expression - mean).reshape(ng, part, 128)
    local_mean = jnp.concatenate(means, axis=1)
    msend[0:1, :] = local_mean

    place = pl.ds(pl.multiple_of(cell * own, own), own)

    def scatter_genes(n):
        to_genes(RSZ, lambda t: ysend.at[t, pl.ds(0, n)], yrecv.at[gene, pl.ds(0, n)])
        yrecv[gene] = ysend[gene]

    def gather_genes(n):
        take(RSZ, yrecv.at[pl.ds(0, ng - 1), pl.ds(0, n)])
        ychunk[0:n, :] = jnp.sum(yrecv[:, 0:n, :], axis=0)
        to_genes(AGZ, lambda t: ychunk.at[pl.ds(0, n)], yfull.at[gene, pl.ds(0, n)])
        yfull[gene, 0:n, :] = ychunk[0:n, :]

    def take_genes(n):
        take(AGZ, yfull.at[pl.ds(0, ng - 1), pl.ds(0, n)])

    def sent_genes(n):
        sent(RSZ, yrecv.at[pl.ds(0, ng - 1), pl.ds(0, n)])
        sent(AGZ, yfull.at[pl.ds(0, ng - 1), pl.ds(0, n)])

    def scatter_cells():
        isend[...] = product(t_parts, yfull[...].reshape(ng * SLOT, k)).reshape(nc, own, k)
        to_cells(RSC, lambda t: isend.at[t], irecv.at[cell])
        irecv[cell] = isend[cell]

    def gather_cells(mine):
        ichunk[...] = mine
        to_cells(AGC, lambda t: ichunk, ifull.at[place])
        ifull[place, :] = mine
        gram = dot(mine, mine, TN)
        for c in range(nc):
            gsend[c] = gram[c * grow : (c + 1) * grow, :]
        to_cells(GRAM_C, lambda t: gsend.at[t], grecv.at[cell])
        grecv[cell] = gsend[cell]

    def gram_genes(turn):
        take(GRAM_C, weight[GRAM_C])
        zsend[...] = jnp.sum(grecv[...], axis=0)
        to_genes(GRAM_Z + turn, lambda t: zsend, zrecv.at[turn, gene])
        zrecv[turn, gene] = zsend[...]

    def gram_cells(turn):
        take(GRAM_Z + turn, zrecv.at[turn, pl.ds(0, ng - 1)])
        csend[...] = jnp.sum(zrecv[turn], axis=0)
        to_cells(GRAM, lambda t: csend, crecv.at[cell])
        crecv[cell] = csend[...]

    def factorise():
        take(GRAM, weight[GRAM])
        for c in range(nc):
            s_ref[c * grow : (c + 1) * grow, :] = crecv[c]
        w_ref[...] = jnp.where(
            lax.broadcasted_iota(jnp.int32, (k, k), 0) == lax.broadcasted_iota(jnp.int32, (k, k), 1), 1.0, 0.0
        )

        def panel(i, carry):
            factor_panel(i, s_ref, w_ref)
            return carry

        lax.fori_loop(0, k // PANEL - 1, panel, 0)
        factor_panel(k // PANEL - 1, s_ref, w_ref, last=True)

    ysend[...] = dot(x_ref[...].reshape(ng * SLOT, cols), prior, NN).reshape(ng, SLOT, k)
    scatter_genes(part + 1)
    to_cells(MEAN, lambda t: msend.at[pl.ds(0, 1)], mrecv.at[cell, pl.ds(0, 1)])
    mrecv[cell, 0:1, :] = local_mean
    take(MEAN, weight[MEAN])
    delta = local_mean - jnp.sum(mrecv[:, 0:1, :], axis=0) * (1.0 / nc)
    dsend[...] = dot(jnp.broadcast_to(delta, (8, cols)), prior, NN)
    to_genes(SHIFT, lambda t: dsend.at[pl.ds(0, 1)], drecv.at[gene, pl.ds(0, 1)])
    drecv[gene, 0:1, :] = dsend[0:1, :]
    x_ref[:, 0:part, :] = x_ref[:, 0:part, :] + delta[None]
    gather_genes(part + 1)
    x = x_ref[...].reshape(ng * SLOT, cols)
    for ref, value in zip(x_parts, split(x)):
        ref[...] = value
    lanes = lax.broadcasted_iota(jnp.int32, (1, ng * SLOT), 1)
    for ref, value in zip(t_parts, split(x.T * jnp.where(lanes % SLOT < part, 1.0 / total, 1.0))):
        ref[...] = value
    take(SHIFT, weight[SHIFT])
    take_genes(part + 1)
    yfull[:, 0:part, :] = yfull[:, 0:part, :] + jnp.sum(drecv[:, 0:1, :], axis=0)[None]
    scatter_cells()
    sent_genes(part + 1)
    take(RSC, weight[RSC])
    gather_cells(jnp.sum(irecv[...], axis=0))

    def to_products():
        take(AGC, weight[AGC])
        ysend[...] = product(x_parts, ifull[...]).reshape(ng, SLOT, k)

    def iteration(step, carry):
        side = lax.rem(step, 2)
        to_products()
        scatter_genes(part + 1)
        gram_genes(side)
        gather_genes(part + 1)
        gram_cells(side)
        take_genes(part + 1)
        sent(RSC, weight[RSC])
        scatter_cells()
        factorise()
        sent_genes(part + 1)
        for kind in (AGC, GRAM_C, GRAM):
            sent(kind, weight[kind])
        sent(GRAM_Z + side, zrecv.at[side, pl.ds(0, ng - 1)])
        take(RSC, weight[RSC])
        gather_cells(dot(jnp.sum(irecv[...], axis=0), w_ref[...], NT))
        return carry

    lax.fori_loop(1, ITERS, iteration, 0)

    to_products()
    last = ITERS % 2
    gram_genes(last)
    scatter_genes(part)
    gram_cells(last)
    gather_genes(part)
    factorise()
    load_ref[...] = dot(ifull[...], w_ref[...], NT) * jnp.sqrt(F32(cols * ng))
    take_genes(part)
    score_ref[...] = dot(yfull[:, 0:part, :].reshape(rows, k), w_ref[...], NT)
    sent_genes(part)
    sent(GRAM_Z + last, zrecv.at[last, pl.ds(0, ng - 1)])
    for kind in (LIB, MEAN, SHIFT, RSC, AGC, GRAM_C, GRAM):
        sent(kind, weight[kind])


def solution(mesh):
    ng, nc = mesh.shape["gene"], mesh.shape["cell"]

    def per_device(counts, prior_basis, prior_values):
        rows, cols = counts.shape
        k = prior_basis.shape[1]
        part, own = rows // ng, cols // nc
        grow = k // nc
        vmem, hbm = pl.BlockSpec(memory_space=pltpu.VMEM), pl.BlockSpec(memory_space=pltpu.HBM)
        scratch = [
            (cols, k), (1, k),
            (ng, SLOT, cols),
            (ng, SLOT, k), (ng, SLOT, k), (SLOT, k), (ng, SLOT, k),
            (8, rows), (ng, 8, rows),
            (8, cols), (nc, 8, cols),
            (8, k), (ng, 8, k),
            (nc, grow, k), (nc, grow, k), (grow, k), (2, ng, grow, k), (grow, k), (nc, grow, k),
            (nc, own, k), (nc, own, k), (own, k), (cols, k),
            (k, k), (k, k),
        ]
        return pl.pallas_call(
            functools.partial(kernel, ng, nc),
            out_shape=(jax.ShapeDtypeStruct((cols, k), F32), jax.ShapeDtypeStruct((rows, k), F32)),
            in_specs=[hbm] * 3,
            out_specs=(vmem, vmem),
            scratch_shapes=[pltpu.VMEM((rows, cols), jnp.int32)]
            + [pltpu.VMEM(s, F32) for s in scratch]
            + [pltpu.VMEM((ng * SLOT, cols), jnp.bfloat16)] * 3
            + [pltpu.VMEM((cols, ng * SLOT), jnp.bfloat16)] * 3
            + [pltpu.SemaphoreType.DMA((KINDS,)), pltpu.SemaphoreType.DMA((KINDS,)), pltpu.SemaphoreType.DMA((3,))],
            compiler_params=pltpu.CompilerParams(
                collective_id=0, has_side_effects=True, vmem_limit_bytes=56_000_000
            ),
        )(counts, prior_basis, prior_values.reshape(1, k))

    return jax.shard_map(
        per_device,
        mesh=mesh,
        in_specs=(P("cell", "gene"), P("gene", None), P()),
        out_specs=(P("gene", None), P("cell", None)),
        check_vma=False,
    )
```
